512 devices in a mesh: row: 16 (over y, x_hi), col: 32 (over x_lo, z, core).
Axes of the slice: x: 4 (x_hi: 2, x_lo: 2; x = x_hi * 2 + x_lo), y: 8, z: 8, core: 2. Of those that a mesh axis runs over, the one named last changes fastest.
Arguments:
- matrix: float32 [8, 16, 128, 4, 32, 128], P(None, 'row', None, None, 'col'), may hold values from -26 to 26, as said below
Outputs:
- banded: float32 [8, 16, 128, 4, 32, 128], P(None, 'row', None, None, 'col')
- reflectors: float32 [8, 16, 128, 128], P(None, 'row')
The draws below stay inside these ranges and needn't reach their ends.
Inputs may be any that keep to these rules, and one draw needn't show every extreme that they name: matrix holds an exactly symmetric matrix: with global indices r and c as in the reference program, A[r, c] equals A[c, r].
All inputs are finite; a program needn't handle non-finite values.
Results may differ from the reference program's by a relative error of at most 0.0003.
Values sent between devices are 32-bit elements; how exact they have to be, the bound alone decides.
No kernel may reach another device: no remote copies, remote signals or barrier semaphores. Data moves between devices by JAX's collectives and lax.ppermute only.
A program may use at most 64 MiB of HBM per device.

```python
import math
import jax
import jax.numpy as jnp
from jax import lax

NB = 128
LC = 4
N = 16384
LR = 8
N_ROW = 16
N_COL = 32


def draw_matrix(key, part):
    key = jax.random.fold_in(key, 11)
    first_key = jax.random.fold_in(key, 0)
    entries = jnp.clip(jax.random.normal(first_key, (N, N), jnp.float32), -6.0, 6.0)
    symmetric = (entries + entries.T) * math.sqrt(0.5)
    return symmetric.reshape(LR, N_ROW, NB, LC, N_COL, NB)


def setup_inputs(seed: int = 0) -> dict:
    splits = jax.random.split(jax.random.key(seed), 2)
    matrix = draw_matrix(jax.random.fold_in(splits[1], 71), 0)
    return {"matrix": matrix}


def product(first, second):
    return jnp.dot(first.astype(jnp.float32), second.astype(jnp.float32), precision=lax.Precision.HIGHEST, preferred_element_type=jnp.float32)

def transposed_product(first, second):
    return lax.dot_general(first.astype(jnp.float32), second.astype(jnp.float32), (((0,), (0,)), ((), ())), precision=lax.Precision.HIGHEST, preferred_element_type=jnp.float32)

def signed_factor(square):
    extent = square.shape[0]
    places = jnp.arange(extent)

    def elimination(column, carry):
        working, chosen = carry
        pivot_value = working[column, column]
        sign_choice = jnp.where(pivot_value >= 0, -1.0, 1.0).astype(square.dtype)
        shifted = pivot_value - sign_choice
        below_mask = places > column
        multipliers = jnp.where(below_mask, working[:, column] / shifted, 0.0)
        reduced = working - jnp.where(below_mask[None, :], multipliers[:, None] * working[column, :][None, :], 0.0)
        reduced = jnp.where(below_mask[:, None] & (places[None, :] == column), multipliers[:, None], reduced)
        reduced = jnp.where((places[:, None] == column) & (places[None, :] == column), shifted, reduced)
        chosen = jnp.where(places == column, sign_choice, chosen)
        return (reduced, chosen)
    working, chosen = lax.fori_loop(0, extent, elimination, (square, jnp.zeros((extent,), square.dtype)))
    upper_factor = jnp.triu(working)
    unit_lower = jnp.tril(working, -1) + jnp.eye(extent, dtype=square.dtype)
    return (upper_factor, chosen, unit_lower)

def compact_factor(upper_factor, chosen, unit_lower):
    scaled = upper_factor * chosen[None, :]
    solved = jax.scipy.linalg.solve_triangular(unit_lower, -scaled.T, lower=True, unit_diagonal=True)
    return solved.T

def reference(matrix):
    block_size = matrix.shape[2]
    extent = matrix.shape[0] * matrix.shape[1] * block_size
    full_matrix = matrix.reshape(extent, extent)
    panel_block = full_matrix[block_size:, :block_size]
    gram_matrix = transposed_product(panel_block, panel_block)
    factor = jnp.linalg.cholesky(gram_matrix)
    orthonormal = jax.scipy.linalg.solve_triangular(factor, panel_block.T, lower=True).T
    upper_factor, chosen, unit_lower = signed_factor(orthonormal[:block_size])
    remainder = jax.scipy.linalg.solve_triangular(upper_factor, orthonormal[block_size:].T, lower=False, trans=1).T
    reflect = jnp.concatenate([jnp.zeros((block_size, block_size), full_matrix.dtype), unit_lower, remainder], axis=0)
    triangle = compact_factor(upper_factor, chosen, unit_lower)
    images = product(full_matrix, reflect)
    positions = jnp.arange(extent)
    images = jnp.where((positions < block_size)[:, None], 0.0, images)
    scaled_images = product(images, triangle)
    coupling = transposed_product(reflect, scaled_images)
    update_rows = scaled_images - 0.5 * product(reflect, product(triangle.T, coupling))
    block_count = extent // block_size

    def update_block(operands):
        block_rows, reflect_rows, wide_rows = operands
        return block_rows - product(reflect_rows, update_rows.T) - product(wide_rows, reflect.T)
    updated = lax.map(update_block, (full_matrix.reshape(block_count, block_size, extent), reflect.reshape(block_count, block_size, block_size), update_rows.reshape(block_count, block_size, block_size)))
    updated = updated.reshape(extent, extent)
    band_block = chosen[:, None] * factor.T
    updated = updated.at[block_size:, :block_size].set(0.0)
    updated = updated.at[block_size:2 * block_size, :block_size].set(band_block)
    updated = updated.at[:block_size, block_size:].set(0.0)
    updated = updated.at[:block_size, block_size:2 * block_size].set(band_block.T)
    return (updated.reshape(matrix.shape), reflect.reshape(matrix.shape[0], matrix.shape[1], block_size, block_size))
```

```python
import functools
import jax
import jax.numpy as jnp
from jax import lax
from jax.experimental import pallas as pl
from jax.experimental.pallas import tpu as pltpu
from jax.sharding import PartitionSpec as P

STEP = 32


def product(first, second, first_dim=1, second_dim=0):
    return lax.dot_general(
        first,
        second,
        (((first_dim,), (second_dim,)), ((), ())),
        precision=lax.Precision.HIGHEST,
        preferred_element_type=jnp.float32,
    )


def factor_kernel(
    gram_ref, second_ref, y_ref, m_ref, t_ref, pair_ref, band_ref, ge, x, e, u, j, sg, *, step
):
    size = gram_ref.shape[0]
    lane = lax.broadcasted_iota(jnp.int32, (step, size), 1)
    lane2 = lax.broadcasted_iota(jnp.int32, (step, 2 * size), 1)
    place = lax.broadcasted_iota(jnp.int32, (step, 1), 0)
    eye = (
        lax.broadcasted_iota(jnp.int32, (size, size), 0)
        == lax.broadcasted_iota(jnp.int32, (size, size), 1)
    ).astype(jnp.float32)
    ge[:, :size] = gram_ref[...]
    ge[:, size:] = eye
    x[:size] = second_ref[...]
    x[size:] = eye
    e[...] = eye
    u[...] = jnp.zeros_like(u)
    j[...] = jnp.zeros_like(j)
    for base in range(0, size, step):
        stop = base + step
        g = ge[base:stop, :]
        w = x[base:stop, :]
        ep = e[base:stop, :]
        f = jnp.where(lane - base == place, 1.0, 0.0).astype(jnp.float32)
        band = jnp.zeros((step, size), jnp.float32)
        sgp = jnp.zeros((step, size), jnp.float32)
        for i in range(step):
            at = base + i
            column = g[:, at : at + 1]
            pivot = g[i : i + 1, at : at + 1]
            root = lax.rsqrt(pivot)
            root = root * (1.5 - 0.5 * pivot * root * root)
            row = jnp.where(lane2[:1] >= at, g[i : i + 1, :] * root, 0.0)
            below = place > i
            here = place == i
            g = jnp.where(here, row, g - jnp.where(below, column * root, 0.0) * row)
            r_row = row[:, :size]
            w_pivot = w[i : i + 1, at : at + 1]
            sign = jnp.where(w_pivot >= 0.0, -1.0, 1.0)
            shifted = w_pivot - sign * (pivot * root)
            inverse = 1.0 / shifted
            s_row = sign * r_row
            t_row = jnp.where(lane[:1] >= at, w[i : i + 1, :], 0.0) - s_row
            l = jnp.where(below, w[:, at : at + 1] * inverse, 0.0)
            w = w - jnp.where(here, s_row, l * t_row)
            w = jnp.where((lane == at) & below, l, w)
            e_row = ep[i : i + 1, :]
            ep = ep - l * e_row
            band = jnp.where(here, s_row, band)
            sgp = jnp.where(here, sign * row[:, size:], sgp)
            f_column = f[:, at : at + 1] * inverse
            f = jnp.where(lane == at, f_column, f - f_column * t_row)
        f = jnp.where((lane >= base) & (lane < stop), f, 0.0)
        u_panel = jnp.where(lane >= base + place, w, 0.0)
        x[base:stop, :] = w
        u[base:stop, :size] = u_panel
        u[base:stop, size:] = ep
        e[base:stop, :] = ep
        band_ref[base:stop, :] = band
        sg[base:stop, :] = sgp
        j[base:stop, :] = f
        if stop < size:
            left = jnp.where(lane >= stop, g[:, :size], 0.0)
            d = product(left, g, 0, 0)
            ge[stop:, :] = ge[stop:, :] - d[stop:, :]
        whole = x[...]
        below_rows = lax.broadcasted_iota(jnp.int32, (2 * size, 1), 0) >= stop
        panel = jnp.where(below_rows | (lax.broadcasted_iota(jnp.int32, (2 * size, 1), 0) >= size), product(whole, j[...]), 0.0)
        d = product(panel, u[...])
        x[...] = whole + panel - d[:, :size]
        if stop < size:
            e[stop:, :] = e[stop:, :] - d[stop:size, size:]
        j[base:stop, :] = jnp.zeros((step, size), jnp.float32)
    rows = lax.broadcasted_iota(jnp.int32, (size, size), 0)
    lanes = lax.broadcasted_iota(jnp.int32, (size, size), 1)
    y_ref[...] = jnp.where(rows > lanes, x[:size], 0.0) + eye
    m = x[size:]
    m = jnp.where(rows <= lanes, m, 0.0)
    m_ref[...] = m
    es = product(e[...], sg[...])
    triangle = -product(u[:, :size], es, 1, 1)
    t_ref[...] = triangle
    pair_ref[:size] = product(m, triangle)
    pair_ref[size:] = -product(product(band_ref[...], m), triangle)


def factors(gram, second):
    size = gram.shape[0]
    square = jax.ShapeDtypeStruct((size, size), jnp.float32)
    return pl.pallas_call(
        functools.partial(factor_kernel, step=STEP),
        out_shape=(square, square, square, jax.ShapeDtypeStruct((2 * size, size), jnp.float32), square),
        scratch_shapes=[
            pltpu.VMEM((size, 2 * size), jnp.float32),
            pltpu.VMEM((2 * size, size), jnp.float32),
            pltpu.VMEM((size, size), jnp.float32),
            pltpu.VMEM((size, 2 * size), jnp.float32),
            pltpu.VMEM((size, size), jnp.float32),
            pltpu.VMEM((size, size), jnp.float32),
        ],
        cost_estimate=pl.CostEstimate(flops=1 << 24, bytes_accessed=1 << 22, transcendentals=1 << 12),
    )(gram, second)


def exchange(array, axis):
    return lax.all_to_all(array, axis, 0, 0)


def gather(array, axis):
    count = lax.axis_size(axis)
    return exchange(jnp.broadcast_to(array[None], (count,) + array.shape), axis)


def to_rows(chunk, column_blocks):
    rows_count = lax.axis_size("row")
    cols_count = lax.axis_size("col")
    ratio = cols_count // rows_count
    parts = cols_count // (ratio * column_blocks)
    pairs = []
    for row in range(rows_count):
        for col in range(cols_count):
            block, part = divmod(col, parts)
            source_row = (block // ratio) * parts + part
            source_col = row + rows_count * (block % ratio)
            pairs.append((source_row * cols_count + source_col, row * cols_count + col))
    return lax.ppermute(chunk, ("row", "col"), pairs)


def on_device(matrix):
    rows_count = lax.axis_size("row")
    cols_count = lax.axis_size("col")
    row_place = lax.axis_index("row")
    col_place = lax.axis_index("col")
    local_blocks = matrix.shape[0]
    size = matrix.shape[2]
    column_blocks = matrix.shape[3]
    rows = local_blocks * size
    cols = column_blocks * size
    local_part = matrix.reshape(rows, cols)
    row_block = jnp.repeat(jnp.arange(local_blocks) * rows_count + row_place, size)
    column_block = jnp.repeat(jnp.arange(column_blocks) * cols_count + col_place, size)
    first = local_part[:, :size]
    corner = local_part[:size, :size]
    mine = rows // cols_count
    thin = size // cols_count
    wide = size // rows_count

    panel = jnp.where((row_block == 0)[:, None], 0.0, first)
    found = exchange(
        jnp.concatenate(
            [
                panel.reshape(cols_count, mine, size),
                product(panel, panel, 0, 0).reshape(cols_count, thin, size),
                jnp.where(row_place == 1, corner, 0.0).reshape(cols_count, thin, size),
            ],
            axis=1,
        ),
        "col",
    )[0]
    square = gather(found[mine:], "row").sum(axis=0)
    found = gather(jnp.concatenate([found[:mine], square], axis=0), "col")
    panel_rows = found[:, :mine].reshape(rows, size)
    gram_matrix = found[:, mine : mine + thin].reshape(size, size)
    second = found[:, mine + thin :].reshape(size, size)
    unit_lower, inverse, triangle, pair, band_block = factors(gram_matrix, second)

    strip = local_part[:size].T.reshape(rows_count, mine, size)
    images = product(local_part, panel_rows, 0, 0).reshape(rows_count, mine, size)
    chunks = exchange(jnp.concatenate([images, strip], axis=1), "row")
    image_chunk = chunks[:, :mine].sum(axis=0)
    chunk_block = (row_place * mine) // size * cols_count + col_place
    panel_chunk = chunks[0, mine:]
    other_chunk = chunks[1, mine:]

    scaled = product(jnp.concatenate([image_chunk, other_chunk], axis=1), pair)
    scaled = jnp.where(chunk_block == 0, 0.0, scaled)
    reflect = product(panel_chunk, inverse)
    reflect = jnp.where(chunk_block == 0, 0.0, reflect)
    lower_piece = lax.dynamic_slice_in_dim(unit_lower, (row_place * mine) % size, mine, axis=0)
    reflect = jnp.where(chunk_block == 1, lower_piece, reflect)

    coupling = product(reflect, scaled, 0, 0).reshape(rows_count, wide, size)
    both = jnp.concatenate([scaled, reflect], axis=0)[None]
    both = jnp.broadcast_to(both, (rows_count, 2 * mine, size))
    found = exchange(jnp.concatenate([both, coupling], axis=1), "row")
    scaled_cols = found[:, :mine].reshape(cols, size)
    reflect_cols = found[:, mine : 2 * mine].reshape(cols, size)
    coupling = found[:, 2 * mine :].sum(axis=0)

    scaled = to_rows(scaled, column_blocks)
    found = gather(jnp.concatenate([scaled, coupling], axis=0), "col")
    scaled_rows = found[:, :mine].reshape(rows, size)
    coupling = gather(found[:, mine:].sum(axis=0), "row").reshape(size, size)
    correction = product(triangle, coupling, 0, 0)

    reflect_rows = product(panel_rows, inverse)
    reflect_rows = jnp.where(
        (row_block == 1)[:, None], jnp.tile(unit_lower, (local_blocks, 1)), reflect_rows
    )
    update_cols = scaled_cols - product(reflect_cols, correction)
    updated = local_part - product(
        jnp.concatenate([reflect_rows, scaled_rows], axis=1),
        jnp.concatenate([update_cols, reflect_cols], axis=1),
        1,
        1,
    )
    left_rim = jnp.where(
        (row_block == 1)[:, None], jnp.tile(band_block, (local_blocks, column_blocks)), 0.0
    )
    banded = jnp.where((column_block == 0)[None, :] & (row_block >= 1)[:, None], left_rim, updated)
    upper_rim = jnp.where(
        (column_block == 1)[None, :], jnp.tile(band_block.T, (local_blocks, column_blocks)), 0.0
    )
    banded = jnp.where((row_block == 0)[:, None] & (column_block >= 1)[None, :], upper_rim, banded)
    return (
        banded.reshape(matrix.shape),
        reflect_rows.reshape(local_blocks, 1, size, size),
    )


def solution(mesh):
    in_specs = (P(None, "row", None, None, "col", None),)
    out_specs = (P(None, "row", None, None, "col", None), P(None, "row", None, None))
    return jax.shard_map(
        on_device, mesh=mesh, in_specs=in_specs, out_specs=out_specs, check_vma=False
    )
```

```python
import functools
import jax
import jax.numpy as jnp
from jax import lax
from jax.experimental import pallas as pl
from jax.experimental.pallas import tpu as pltpu
from jax.sharding import PartitionSpec as P

STEP = 32


def product(first, second, first_dim=1, second_dim=0):
    return lax.dot_general(
        first,
        second,
        (((first_dim,), (second_dim,)), ((), ())),
        precision=lax.Precision.HIGHEST,
        preferred_element_type=jnp.float32,
    )


def halves(array):
    high = array.astype(jnp.bfloat16)
    return high, (array - high.astype(jnp.float32)).astype(jnp.bfloat16)


def passes(first, second, first_dim=1, second_dim=0):
    dims = (((first_dim,), (second_dim,)), ((), ()))

    def one(a, b):
        return lax.dot_general(a, b, dims, preferred_element_type=jnp.float32)

    return one(first[0], second[0]) + (one(first[0], second[1]) + one(first[1], second[0]))


def factor_kernel(own_ref, other_ref, out_ref, ge, x, e, u, j, sg, bd, *, step):
    size = out_ref.shape[1]
    thin = size // own_ref.shape[0]
    mine = own_ref.shape[1] - 2 * thin
    lane = lax.broadcasted_iota(jnp.int32, (step, size), 1)
    lane2 = lax.broadcasted_iota(jnp.int32, (step, 2 * size), 1)
    place = lax.broadcasted_iota(jnp.int32, (step, 1), 0)
    eye = (
        lax.broadcasted_iota(jnp.int32, (size, size), 0)
        == lax.broadcasted_iota(jnp.int32, (size, size), 1)
    ).astype(jnp.float32)
    both = own_ref[:, mine:, :] + other_ref[:, mine:, :]
    ge[:, :size] = both[:, :thin].reshape(size, size)
    x[:size] = both[:, thin:].reshape(size, size)
    ge[:, size:] = eye
    x[size:] = eye
    e[...] = eye
    u[...] = jnp.zeros_like(u)
    j[...] = jnp.zeros_like(j)
    for base in range(0, size, step):
        stop = base + step
        g = ge[base:stop, :]
        w = x[base:stop, :]
        ep = e[base:stop, :]
        f = jnp.where(lane - base == place, 1.0, 0.0).astype(jnp.float32)
        band = jnp.zeros((step, size), jnp.float32)
        sgp = jnp.zeros((step, size), jnp.float32)
        for i in range(step):
            at = base + i
            column = g[:, at : at + 1]
            pivot = g[i : i + 1, at : at + 1]
            root = lax.rsqrt(pivot)
            root = root * (1.5 - 0.5 * pivot * root * root)
            row = jnp.where(lane2[:1] >= at, g[i : i + 1, :] * root, 0.0)
            below = place > i
            here = place == i
            g = jnp.where(here, row, g - jnp.where(below, column * root, 0.0) * row)
            r_row = row[:, :size]
            w_pivot = w[i : i + 1, at : at + 1]
            sign = jnp.where(w_pivot >= 0.0, -1.0, 1.0)
            shifted = w_pivot - sign * (pivot * root)
            inverse = 1.0 / shifted
            s_row = sign * r_row
            t_row = jnp.where(lane[:1] >= at, w[i : i + 1, :], 0.0) - s_row
            l = jnp.where(below, w[:, at : at + 1] * inverse, 0.0)
            w = w - jnp.where(here, s_row, l * t_row)
            w = jnp.where((lane == at) & below, l, w)
            e_row = ep[i : i + 1, :]
            ep = ep - l * e_row
            band = jnp.where(here, s_row, band)
            sgp = jnp.where(here, sign * row[:, size:], sgp)
            f_column = f[:, at : at + 1] * inverse
            f = jnp.where(lane == at, f_column, f - f_column * t_row)
        f = jnp.where((lane >= base) & (lane < stop), f, 0.0)
        u_panel = jnp.where(lane >= base + place, w, 0.0)
        x[base:stop, :] = w
        u[base:stop, :size] = u_panel
        u[base:stop, size:] = ep
        e[base:stop, :] = ep
        bd[base:stop, :] = band
        sg[base:stop, :] = sgp
        j[base:stop, :] = f
        if stop < size:
            left = jnp.where(lane >= stop, g[:, :size], 0.0)
            d = product(left, g, 0, 0)
            ge[stop:, :] = ge[stop:, :] - d[stop:, :]
        whole = x[...]
        below_rows = lax.broadcasted_iota(jnp.int32, (2 * size, 1), 0) >= stop
        panel = jnp.where(below_rows | (lax.broadcasted_iota(jnp.int32, (2 * size, 1), 0) >= size), product(whole, j[...]), 0.0)
        d = product(panel, u[...])
        x[...] = whole + panel - d[:, :size]
        if stop < size:
            e[stop:, :] = e[stop:, :] - d[stop:size, size:]
        j[base:stop, :] = jnp.zeros((step, size), jnp.float32)
    rows = lax.broadcasted_iota(jnp.int32, (size, size), 0)
    lanes = lax.broadcasted_iota(jnp.int32, (size, size), 1)
    m = jnp.where(rows <= lanes, x[size:], 0.0)
    es = product(e[...], sg[...])
    triangle = -product(u[:, :size], es, 1, 1)
    out_ref[:size] = product(m, triangle)
    out_ref[size : 2 * size] = -product(product(bd[...], m), triangle)
    out_ref[2 * size : 3 * size] = m
    out_ref[3 * size : 4 * size] = jnp.where(rows > lanes, x[:size], 0.0) + eye
    out_ref[4 * size : 5 * size] = triangle
    out_ref[5 * size :] = bd[...]


def open_kernel(place, own_ref, other_ref, out_ref):
    size = own_ref.shape[1]
    count, extent, _ = out_ref.shape
    thin = size // count
    mine = extent - 2 * thin
    core = place[1]
    panel = jnp.where(core == 0, own_ref[...], other_ref[...])
    second = jnp.where((place[0] == 1) & (core == 0), panel[:size], 0.0)
    index = lax.broadcasted_iota(jnp.int32, panel.shape, 0)
    panel = jnp.where((index < size) & (place[0] == 0) & (core == 0), 0.0, panel)
    out_ref[:, :mine, :] = panel.reshape(count, mine, size)
    out_ref[:, mine : mine + thin, :] = product(panel, panel, 0, 0).reshape(count, thin, size)
    out_ref[:, mine + thin :, :] = second.reshape(count, thin, size)


def strip_kernel(place, strip_ref, out_ref):
    size = strip_ref.shape[2]
    count, mine, _ = out_ref.shape
    each = size // mine
    for b in range(strip_ref.shape[1]):
        turned = strip_ref[:, b, :].T
        if b == 0:
            turned = jnp.where(place[1] == 0, 0.0, turned)
        out_ref[b * each : (b + 1) * each] = turned.reshape(each, mine, size)


def image_kernel(place, own_ref, other_ref, matrix_ref, chunk_ref, out_ref):
    size = own_ref.shape[2]
    count, extent, _ = out_ref.shape
    mine = extent // 2
    each = size // mine
    own = own_ref[:, :mine, :].reshape(-1, size)
    other = other_ref[:, :mine, :].reshape(-1, size)
    even = place[1] % 2 == 0
    panel = jnp.concatenate([jnp.where(even, own, other), jnp.where(even, other, own)], axis=0)
    high, low = halves(panel.T)
    matrix_high, matrix_low = halves(matrix_ref[...])
    image = jnp.dot(
        jnp.concatenate([high, low], axis=0), matrix_high, preferred_element_type=jnp.float32
    )
    image = image[:size] + (
        image[size:] + jnp.dot(high, matrix_low, preferred_element_type=jnp.float32)
    )
    for b in range(matrix_ref.shape[1] // size):
        turned = image[:, b * size : (b + 1) * size].T
        out_ref[b * each : (b + 1) * each, :mine, :] = turned.reshape(each, mine, size)
    out_ref[:, mine:, :] = jnp.broadcast_to(chunk_ref[...][None], (count, mine, size))


def middle_kernel(place, found_ref, panel_ref, second_ref, factors_ref, out_ref):
    size = factors_ref.shape[1]
    count, extent, _ = found_ref.shape
    mine = extent // 2
    wide = size // count
    image = found_ref[0, :mine, :]
    for p in range(1, count):
        image = image + found_ref[p, :mine, :]
    block = (place[0] * mine) // size * place[3] + place[1]
    both = jnp.concatenate([image, second_ref[...]], axis=1)
    scaled = product(both, factors_ref[: 2 * size])
    scaled = jnp.where(block == 0, 0.0, scaled)
    reflect = product(panel_ref[...], factors_ref[2 * size : 3 * size])
    offset = pl.multiple_of(3 * size + (place[0] * mine) % size, mine)
    reflect = jnp.where(block == 1, factors_ref[pl.ds(offset, mine), :], reflect)
    reflect = jnp.where(block == 0, 0.0, reflect)
    coupling = product(reflect, scaled, 0, 0)
    out_ref[:, :mine, :] = jnp.broadcast_to(scaled[None], (count, mine, size))
    out_ref[:, mine:, :] = coupling.reshape(count, wide, size)


def close_kernel(
    place,
    matrix_ref,
    cols_ref,
    reflect_cols_ref,
    own_ref,
    other_ref,
    coupling_ref,
    reflect_ref,
    factors_ref,
    out_ref,
    high,
    low,
):
    step = pl.program_id(0)
    size = factors_ref.shape[1]
    mine = cols_ref.shape[1] - coupling_ref.shape[1]
    blocks = out_ref.shape[1]
    extent = out_ref.shape[0]
    ratio = extent // size
    each = extent // mine

    @pl.when(step == 0)
    def _():
        coupling = coupling_ref[...].reshape(size, size)
        correction = product(factors_ref[4 * size : 5 * size], coupling, 0, 0)
        reflect_cols = reflect_cols_ref[...]
        scaled_cols = cols_ref[:, :mine, :].reshape(-1, size)
        update = scaled_cols - passes(halves(reflect_cols), halves(correction))
        right = halves(jnp.concatenate([update, reflect_cols], axis=1))
        high[...] = right[0]
        low[...] = right[1]

    pairs = own_ref.shape[0]
    first = pl.multiple_of((step * each) % pairs, each)
    here = (step * each) // pairs == place[1] % 2
    scaled = jnp.where(
        here, own_ref[pl.ds(first, each), :mine, :], other_ref[pl.ds(first, each), :mine, :]
    )
    rows = pl.ds(pl.multiple_of(step * extent, extent), extent)
    left = jnp.concatenate([reflect_ref[rows, :], scaled.reshape(extent, size)], axis=1)
    value = matrix_ref[rows, :] - passes(halves(left), (high[...], low[...]), 1, 1)
    band = factors_ref[5 * size :]
    for h in range(ratio):
        row_block = (step * ratio + h) * place[2] + place[0]
        for b in range(blocks):
            column_block = b * place[3] + place[1]
            part = slice(h * size, (h + 1) * size)
            tile = value[part, b * size : (b + 1) * size]
            if b == 0:
                rim = jnp.where(row_block == 1, band, 0.0)
                tile = jnp.where((column_block == 0) & (row_block >= 1), rim, tile)
            if h == 0:
                rim = jnp.where(column_block == 1, band.T, 0.0) if b == 0 else jnp.zeros_like(band)
                tile = jnp.where((row_block == 0) & (column_block >= 1), rim, tile)
            out_ref[part, b, :] = tile


def cost(flops, moved):
    return pl.CostEstimate(flops=flops, bytes_accessed=moved, transcendentals=0)


def struct(*shape):
    return jax.ShapeDtypeStruct(shape, jnp.float32)


SCALARS = pl.BlockSpec(memory_space=pltpu.SMEM)
WHOLE = pl.BlockSpec(memory_space=pltpu.VMEM)
ROOM = pltpu.CompilerParams(vmem_limit_bytes=16 << 20)


def factors(own, other):
    size = own.shape[2]
    return pl.pallas_call(
        functools.partial(factor_kernel, step=STEP),
        out_shape=struct(6 * size, size),
        scratch_shapes=[
            pltpu.VMEM((size, 2 * size), jnp.float32),
            pltpu.VMEM((2 * size, size), jnp.float32),
            pltpu.VMEM((size, size), jnp.float32),
            pltpu.VMEM((size, 2 * size), jnp.float32),
            pltpu.VMEM((size, size), jnp.float32),
            pltpu.VMEM((size, size), jnp.float32),
            pltpu.VMEM((size, size), jnp.float32),
        ],
        compiler_params=ROOM,
        cost_estimate=cost(1 << 28, 1 << 25),
    )(own, other)


def exchange(array):
    return lax.all_to_all(array, "row", 0, 0)


def same_core(array):
    count = lax.axis_size("col")
    groups = [list(range(core, count, 2)) for core in range(2)]
    return lax.all_to_all(array, "col", 0, 0, axis_index_groups=groups)


def flip(array):
    count = lax.axis_size("col")
    return lax.ppermute(array, "col", [(i, i ^ 1) for i in range(count)])


def to_all(array, count):
    return jnp.broadcast_to(array[None], (count,) + array.shape)


def to_rows(chunk, column_blocks):
    rows_count = lax.axis_size("row")
    cols_count = lax.axis_size("col")
    ratio = cols_count // rows_count
    parts = cols_count // (ratio * column_blocks)
    pairs = []
    for row in range(rows_count):
        for col in range(cols_count):
            block, part = divmod(col % 2 * (cols_count // 2) + col // 2, parts)
            source_row = (block // ratio) * parts + part
            source_col = row + rows_count * (block % ratio)
            pairs.append((source_row * cols_count + source_col, row * cols_count + col))
    return lax.ppermute(chunk, ("row", "col"), pairs)


def on_device(matrix):
    rows_count = lax.axis_size("row")
    cols_count = lax.axis_size("col")
    row_place = lax.axis_index("row")
    col_place = lax.axis_index("col")
    local_blocks = matrix.shape[0]
    size = matrix.shape[2]
    column_blocks = matrix.shape[3]
    rows = local_blocks * size
    cols = column_blocks * size
    ratio = cols_count // rows_count
    pairs = cols_count // 2
    mine = rows // cols_count
    thin = size // pairs
    wide = size // rows_count
    table = matrix.reshape(rows, column_blocks, size)
    local_part = matrix.reshape(rows, cols)
    place = jnp.stack(
        [row_place, col_place, jnp.int32(rows_count), jnp.int32(cols_count)]
    ).astype(jnp.int32)

    panel = table[:, 0, :]
    opening = pl.pallas_call(
        open_kernel,
        out_shape=struct(pairs, mine + 2 * thin, size),
        in_specs=[SCALARS, WHOLE, WHOLE],
        compiler_params=ROOM,
        cost_estimate=cost(rows * size * size, 8 * rows * size),
    )(place, panel[: rows // 2], lax.ppermute(panel[rows // 2 :], "col", [(0, 1)]))
    found = same_core(opening)[0]
    strip = pl.pallas_call(
        strip_kernel,
        grid=(1,),
        out_shape=struct(rows_count, mine, size),
        in_specs=[SCALARS, pl.BlockSpec((size, column_blocks, size), lambda i: (0, 0, 0))],
        compiler_params=ROOM,
        cost_estimate=cost(0, 8 * size * cols),
    )(place, table)
    summed = exchange(jnp.concatenate([strip, to_all(found[mine:], rows_count)], axis=1))
    panel_chunk = summed[0, :mine]
    second_chunk = summed[1, :mine]
    square = summed[:, mine:].sum(axis=0)
    own = same_core(to_all(jnp.concatenate([found[:mine], square], axis=0), pairs))
    other = flip(own)

    images = pl.pallas_call(
        image_kernel,
        out_shape=struct(rows_count, 2 * mine, size),
        in_specs=[SCALARS, WHOLE, WHOLE, WHOLE, WHOLE],
        compiler_params=ROOM,
        cost_estimate=cost(2 * rows * cols * size, 4 * rows * (cols + 3 * size)),
    )(place, own, other, local_part, panel_chunk)
    chunks = exchange(images)
    packed = factors(own, other)

    middle = pl.pallas_call(
        middle_kernel,
        out_shape=struct(rows_count, mine + wide, size),
        in_specs=[SCALARS, WHOLE, WHOLE, WHOLE, WHOLE],
        compiler_params=ROOM,
        cost_estimate=cost(2 * mine * size * size * 5, 8 * rows * size),
    )(place, chunks, panel_chunk, second_chunk, packed)
    scaled = to_rows(middle[0, :mine], column_blocks)
    at_cols = exchange(middle)
    coupling = at_cols[:, mine:].sum(axis=0)

    part = same_core(to_all(jnp.concatenate([scaled, coupling], axis=0), pairs))
    rest = flip(part)
    coupling = (part[:, mine:] + rest[:, mine:]).sum(axis=0)
    coupling = exchange(to_all(coupling, rows_count))

    even = col_place % 2 == 0
    own_rows = own[:, :mine].reshape(rows // 2, size)
    other_rows = other[:, :mine].reshape(rows // 2, size)
    panel_rows = jnp.concatenate(
        [jnp.where(even, own_rows, other_rows), jnp.where(even, other_rows, own_rows)], axis=0
    )
    inverse = packed[2 * size : 3 * size]
    unit_lower = packed[3 * size : 4 * size]
    row_block = jnp.repeat(jnp.arange(local_blocks) * rows_count + row_place, size)
    reflect_rows = jnp.where(
        (row_block == 1)[:, None],
        jnp.tile(unit_lower, (local_blocks, 1)),
        product(panel_rows, inverse),
    )
    column_block = jnp.repeat(jnp.arange(column_blocks) * cols_count + col_place, size)
    reflect_cols = jnp.where(
        (column_block == 1)[:, None],
        jnp.tile(unit_lower, (column_blocks, 1)),
        product(chunks[:, mine:].reshape(cols, size), inverse),
    )
    banded = pl.pallas_call(
        close_kernel,
        grid=(column_blocks,),
        out_shape=struct(rows, column_blocks, size),
        in_specs=[SCALARS] + [WHOLE] * 8,
        out_specs=pl.BlockSpec((ratio * size, column_blocks, size), lambda i: (i, 0, 0)),
        scratch_shapes=[
            pltpu.VMEM((cols, 2 * size), jnp.bfloat16),
            pltpu.VMEM((cols, 2 * size), jnp.bfloat16),
        ],
        compiler_params=ROOM,
        cost_estimate=cost(4 * rows * cols * size, 8 * rows * cols),
    )(place, local_part, at_cols, reflect_cols, part, rest, coupling, reflect_rows, packed)
    return (
        banded.reshape(matrix.shape),
        reflect_rows.reshape(local_blocks, 1, size, size),
    )


def solution(mesh):
    in_specs = (P(None, "row", None, None, "col", None),)
    out_specs = (P(None, "row", None, None, "col", None), P(None, "row", None, None))
    return jax.shard_map(
        on_device, mesh=mesh, in_specs=in_specs, out_specs=out_specs, check_vma=False
    )
```

```python
import functools
import jax
import jax.numpy as jnp
from jax import lax
from jax.experimental import pallas as pl
from jax.experimental.pallas import tpu as pltpu
from jax.sharding import PartitionSpec as P

CLOSING = 2


def product(first, second, first_dim=1, second_dim=0):
    return lax.dot_general(
        first,
        second,
        (((first_dim,), (second_dim,)), ((), ())),
        precision=lax.Precision.HIGHEST,
        preferred_element_type=jnp.float32,
    )


def halves(array):
    high = array.astype(jnp.bfloat16)
    return high, (array - high.astype(jnp.float32)).astype(jnp.bfloat16)


def passes(first, second, first_dim=1, second_dim=0):
    dims = (((first_dim,), (second_dim,)), ((), ()))

    def one(a, b):
        return lax.dot_general(a, b, dims, preferred_element_type=jnp.float32)

    return one(first[0], second[0]) + (one(first[0], second[1]) + one(first[1], second[0]))


def factor_kernel(base_ref, out_ref):
    size = base_ref.shape[1]
    lane = lax.broadcasted_iota(jnp.int32, (1, size), 1)
    lane2 = lax.broadcasted_iota(jnp.int32, (1, 2 * size), 1)
    place = lax.broadcasted_iota(jnp.int32, (size, 1), 0)
    eye = (lane == place).astype(jnp.float32)
    g = jnp.concatenate([base_ref[:size], eye], axis=1)
    w = base_ref[size:]
    e = eye
    m = eye
    band = jnp.zeros((size, size), jnp.float32)
    turned = jnp.zeros((size, size), jnp.float32)
    for i in range(size):
        below = place > i
        here = place == i
        pivot = g[i : i + 1, i : i + 1]
        root = lax.rsqrt(pivot)
        root = root * (1.5 - 0.5 * pivot * root * root)
        row = jnp.where(lane2 >= i, g[i : i + 1, :] * root, 0.0)
        g = g - jnp.where(below, g[:, i : i + 1] * root, 0.0) * row
        r_row = row[:, :size]
        w_pivot = w[i : i + 1, i : i + 1]
        sign = jnp.where(w_pivot >= 0.0, -1.0, 1.0)
        inverse = 1.0 / (w_pivot - sign * (pivot * root))
        s_row = sign * r_row
        t_row = jnp.where(lane >= i, w[i : i + 1, :], 0.0) - s_row
        l = jnp.where(below, w[:, i : i + 1] * inverse, 0.0)
        w = w - jnp.where(here, s_row, l * t_row)
        w = jnp.where((lane == i) & below, l, w)
        e = e - l * e[i : i + 1, :]
        band = jnp.where(here, s_row, band)
        turned = jnp.where(here, sign * row[:, size:], turned)
        m_column = m[:, i : i + 1] * inverse
        m = jnp.where(lane == i, m_column, m - m_column * t_row)
    upper = jnp.where(lane >= place, w, 0.0)
    triangle = -product(upper, product(e, turned), 1, 1)
    out_ref[:size] = product(m, triangle)
    out_ref[size : 2 * size] = -product(product(band, m), triangle)
    out_ref[2 * size : 3 * size] = m
    out_ref[3 * size : 4 * size] = jnp.where(place > lane, w, 0.0) + eye
    out_ref[4 * size : 5 * size] = triangle
    out_ref[5 * size :] = band


def open_kernel(place, own_ref, other_ref, out_ref):
    size = own_ref.shape[1]
    count, extent, _ = out_ref.shape
    thin = size // count
    mine = extent - 2 * thin
    core = place[1]
    panel = jnp.where(core == 0, own_ref[...], other_ref[...])
    second = jnp.where((place[0] == 1) & (core == 0), panel[:size], 0.0)
    index = lax.broadcasted_iota(jnp.int32, panel.shape, 0)
    panel = jnp.where((index < size) & (place[0] == 0) & (core == 0), 0.0, panel)
    out_ref[:, :mine, :] = panel.reshape(count, mine, size)
    out_ref[:, mine : mine + thin, :] = product(panel, panel, 0, 0).reshape(count, thin, size)
    out_ref[:, mine + thin :, :] = second.reshape(count, thin, size)


def strip_kernel(place, matrix_ref, table_ref, out_ref):
    size = matrix_ref.shape[2]
    blocks = matrix_ref.shape[1]
    count, mine, _ = out_ref.shape
    each = size // mine
    for b in range(blocks):
        table_ref[:, b * size : (b + 1) * size] = matrix_ref[:, b, :]

    @pl.when(pl.program_id(0) == 0)
    def _():
        for b in range(blocks):
            turned = matrix_ref[:size, b, :].T
            if b == 0:
                turned = jnp.where(place[1] == 0, 0.0, turned)
            out_ref[b * each : (b + 1) * each] = turned.reshape(each, mine, size)


def image_kernel(
    place, own_ref, other_ref, matrix_ref, chunk_ref, out_ref, panel_ref, base_ref
):
    size = own_ref.shape[2]
    count, extent, _ = out_ref.shape
    mine = extent // 2
    each = size // mine
    own = own_ref[:, :mine, :].reshape(-1, size)
    other = other_ref[:, :mine, :].reshape(-1, size)
    even = place[1] % 2 == 0
    panel = jnp.concatenate([jnp.where(even, own, other), jnp.where(even, other, own)], axis=0)
    panel_ref[...] = panel
    both = own_ref[:, mine:, :] + other_ref[:, mine:, :]
    thin = both.shape[1] // 2
    base_ref[:size] = both[:, :thin].reshape(size, size)
    base_ref[size:] = both[:, thin:].reshape(size, size)
    high, low = halves(panel.T)
    matrix_high, matrix_low = halves(matrix_ref[...])
    image = jnp.dot(
        jnp.concatenate([high, low], axis=0), matrix_high, preferred_element_type=jnp.float32
    )
    image = image[:size] + (
        image[size:] + jnp.dot(high, matrix_low, preferred_element_type=jnp.float32)
    )
    for b in range(matrix_ref.shape[1] // size):
        turned = image[:, b * size : (b + 1) * size].T
        out_ref[b * each : (b + 1) * each, :mine, :] = turned.reshape(each, mine, size)
    out_ref[:, mine:, :] = jnp.broadcast_to(chunk_ref[...][None], (count, mine, size))


def middle_kernel(place, found_ref, panel_ref, second_ref, factors_ref, out_ref, scaled_ref):
    size = factors_ref.shape[1]
    count, extent, _ = found_ref.shape
    mine = extent // 2
    wide = size // count
    image = found_ref[0, :mine, :]
    for p in range(1, count):
        image = image + found_ref[p, :mine, :]
    block = (place[0] * mine) // size * place[3] + place[1]
    both = jnp.concatenate([image, second_ref[...]], axis=1)
    scaled = product(both, factors_ref[: 2 * size])
    scaled = jnp.where(block == 0, 0.0, scaled)
    reflect = product(panel_ref[...], factors_ref[2 * size : 3 * size])
    offset = pl.multiple_of(3 * size + (place[0] * mine) % size, mine)
    reflect = jnp.where(block == 1, factors_ref[pl.ds(offset, mine), :], reflect)
    reflect = jnp.where(block == 0, 0.0, reflect)
    coupling = product(reflect, scaled, 0, 0)
    scaled_ref[...] = scaled
    out_ref[:, :mine, :] = jnp.broadcast_to(scaled[None], (count, mine, size))
    out_ref[:, mine:, :] = coupling.reshape(count, wide, size)


def gather_kernel(found_ref, other_ref, scaled_ref, out_ref):
    mine = scaled_ref.shape[0]
    count = out_ref.shape[0]
    out_ref[:, :mine, :] = jnp.broadcast_to(scaled_ref[...][None], (count,) + scaled_ref.shape)
    pieces = found_ref[:, mine:, :].sum(axis=0) + other_ref[...]
    out_ref[:, mine:, :] = jnp.broadcast_to(pieces[None], (count,) + pieces.shape)


def coupling_kernel(part_ref, out_ref, scaled_ref):
    mine = scaled_ref.shape[1]
    pieces = part_ref[:, mine:, :].sum(axis=0)
    out_ref[...] = jnp.broadcast_to(pieces[None], out_ref.shape)
    scaled_ref[...] = part_ref[:, :mine, :]


def reflect_kernel(place, panel_ref, chunks_ref, factors_ref, ready_ref, rows_ref, cols_ref):
    del ready_ref
    size = factors_ref.shape[1]
    mine = chunks_ref.shape[1] // 2
    inverse = factors_ref[2 * size : 3 * size]
    unit_lower = factors_ref[3 * size : 4 * size]
    rows_ref[...] = product(panel_ref[...], inverse)
    cols_ref[...] = product(chunks_ref[:, mine:, :].reshape(-1, size), inverse)

    @pl.when(place[0] == 1)
    def _():
        rows_ref[:size] = unit_lower

    @pl.when(place[1] == 1)
    def _():
        cols_ref[:size] = unit_lower


def close_kernel(
    place,
    matrix_ref,
    cols_ref,
    reflect_cols_ref,
    own_ref,
    other_ref,
    coupling_ref,
    reflect_ref,
    triangle_ref,
    band_ref,
    out_ref,
    high,
    low,
):
    step = pl.program_id(0)
    size = band_ref.shape[1]
    mine = own_ref.shape[1]
    blocks = out_ref.shape[1]
    extent = out_ref.shape[0]
    parts = size // mine
    pairs, count = own_ref.shape[0], cols_ref.shape[0]
    ratio = 2 * pairs // count

    @pl.when(step == 0)
    def _():
        coupling = coupling_ref[...].reshape(size, size)
        correction = product(triangle_ref[...], coupling, 0, 0)
        reflect_cols = reflect_cols_ref[...]
        scaled_cols = cols_ref[:, :mine, :].reshape(-1, size)
        update = scaled_cols - passes(halves(reflect_cols), halves(correction))
        right = halves(jnp.concatenate([update, reflect_cols], axis=1))
        high[...] = right[0]
        low[...] = right[1]

    scaled = []
    for k in range(extent // mine):
        block, part = divmod(k, parts)
        source = (step * (extent // size // ratio) + block // ratio) * parts + part
        col = block % ratio * count + lax.rem(source + count // 2, count)
        here = lax.rem(col, 2) == lax.rem(place[1], 2)
        at = lax.div(col, 2)
        scaled.append(jnp.where(here, own_ref[at], other_ref[at]))
    left = jnp.concatenate([reflect_ref[...], jnp.concatenate(scaled, axis=0)], axis=1)
    value = matrix_ref[...] - passes(halves(left), (high[...], low[...]), 1, 1)
    band = band_ref[...]
    for h in range(extent // size):
        row_block = (step * (extent // size) + h) * place[2] + place[0]
        for b in range(blocks):
            column_block = b * place[3] + place[1]
            tile = value[h * size : (h + 1) * size, b * size : (b + 1) * size]
            if b == 0:
                rim = jnp.where(row_block == 1, band, 0.0)
                tile = jnp.where((column_block == 0) & (row_block >= 1), rim, tile)
            if h == 0:
                rim = jnp.where(column_block == 1, band.T, 0.0) if b == 0 else jnp.zeros_like(band)
                tile = jnp.where((row_block == 0) & (column_block >= 1), rim, tile)
            out_ref[h * size : (h + 1) * size, b, :] = tile


def cost(flops, moved):
    return pl.CostEstimate(flops=flops, bytes_accessed=moved, transcendentals=0)


def struct(*shape):
    return jax.ShapeDtypeStruct(shape, jnp.float32)


SCALARS = pl.BlockSpec(memory_space=pltpu.SMEM)
WHOLE = pl.BlockSpec(memory_space=pltpu.VMEM)


def entire(array):
    return pl.BlockSpec(array.shape, lambda i: (0,) * array.ndim)


ROOM = pltpu.CompilerParams(vmem_limit_bytes=24 << 20)
MORE = pltpu.CompilerParams(vmem_limit_bytes=56 << 20)


def factors(base):
    size = base.shape[1]
    return pl.pallas_call(
        factor_kernel,
        out_shape=struct(6 * size, size),
        compiler_params=ROOM,
        cost_estimate=cost(1 << 28, 1 << 25),
    )(base)


def exchange(array):
    return lax.all_to_all(array, "row", 0, 0)


def same_core(array):
    count = lax.axis_size("col")
    groups = [list(range(core, count, 2)) for core in range(2)]
    return lax.all_to_all(array, "col", 0, 0, axis_index_groups=groups)


def flip(array):
    count = lax.axis_size("col")
    return lax.ppermute(array, "col", [(i, i ^ 1) for i in range(count)])


def to_all(array, count):
    return jnp.broadcast_to(array[None], (count,) + array.shape)


def to_rows(chunk):
    rows_count = lax.axis_size("row")
    cols_count = lax.axis_size("col")
    pairs = []
    for row in range(rows_count):
        for col in range(cols_count):
            half, k = divmod(col, rows_count)
            source = (k + rows_count // 2) % rows_count * cols_count + half * rows_count + row
            pairs.append((source, row * cols_count + col))
    return lax.ppermute(chunk, ("row", "col"), pairs)


def on_device(matrix):
    rows_count = lax.axis_size("row")
    cols_count = lax.axis_size("col")
    row_place = lax.axis_index("row")
    col_place = lax.axis_index("col")
    local_blocks = matrix.shape[0]
    size = matrix.shape[2]
    column_blocks = matrix.shape[3]
    rows = local_blocks * size
    cols = column_blocks * size
    ratio = cols_count // rows_count
    pairs = cols_count // 2
    mine = rows // cols_count
    thin = size // pairs
    wide = size // rows_count
    table = matrix.reshape(rows, column_blocks, size)
    place = jnp.stack(
        [row_place, col_place, jnp.int32(rows_count), jnp.int32(cols_count)]
    ).astype(jnp.int32)

    panel = table[:, 0, :]
    opening = pl.pallas_call(
        open_kernel,
        out_shape=struct(pairs, mine + 2 * thin, size),
        in_specs=[SCALARS, WHOLE, WHOLE],
        compiler_params=ROOM,
        cost_estimate=cost(rows * size * size, 8 * rows * size),
    )(place, panel[: rows // 2], lax.ppermute(panel[rows // 2 :], "col", [(0, 1)]))
    found = same_core(opening)[0]
    local_part, strip = pl.pallas_call(
        strip_kernel,
        grid=(column_blocks,),
        out_shape=(struct(rows, cols), struct(rows_count, mine, size)),
        in_specs=[
            SCALARS,
            pl.BlockSpec((rows // column_blocks, column_blocks, size), lambda i: (i, 0, 0)),
        ],
        out_specs=(
            pl.BlockSpec((rows // column_blocks, cols), lambda i: (i, 0)),
            pl.BlockSpec((rows_count, mine, size), lambda i: (0, 0, 0)),
        ),
        compiler_params=ROOM,
        cost_estimate=cost(0, 8 * rows * cols),
    )(place, table)
    summed = exchange(jnp.concatenate([strip, to_all(found[mine:], rows_count)], axis=1))
    panel_chunk = summed[0, :mine]
    second_chunk = summed[1, :mine]
    square = summed[:, mine:].sum(axis=0)
    own = same_core(to_all(jnp.concatenate([found[:mine], square], axis=0), pairs))
    other = flip(own)

    images, panel_rows, base = pl.pallas_call(
        image_kernel,
        out_shape=(struct(rows_count, 2 * mine, size), struct(rows, size), struct(2 * size, size)),
        in_specs=[SCALARS, WHOLE, WHOLE, WHOLE, WHOLE],
        compiler_params=ROOM,
        cost_estimate=cost(2 * rows * cols * size, 4 * rows * (cols + 3 * size)),
    )(place, own, other, local_part, panel_chunk)
    chunks = exchange(images)
    packed = factors(base)

    middle, scaled = pl.pallas_call(
        middle_kernel,
        out_shape=(struct(rows_count, mine + wide, size), struct(mine, size)),
        in_specs=[SCALARS, WHOLE, WHOLE, WHOLE, WHOLE],
        compiler_params=ROOM,
        cost_estimate=cost(2 * mine * size * size * 5, 8 * rows * size),
    )(place, chunks, panel_chunk, second_chunk, packed)
    scaled = to_rows(scaled)
    at_cols = exchange(middle)

    gathering = pl.pallas_call(
        gather_kernel,
        out_shape=struct(pairs, mine + wide, size),
        compiler_params=ROOM,
        cost_estimate=cost(0, 4 * rows * size),
    )(at_cols, flip(at_cols[:, mine:].sum(axis=0)), scaled)
    part = same_core(gathering)
    coupling, part = pl.pallas_call(
        coupling_kernel,
        out_shape=(struct(rows_count, wide, size), struct(pairs, mine, size)),
        compiler_params=ROOM,
        cost_estimate=cost(0, 4 * rows * size),
    )(part)
    reflect_rows, reflect_cols = pl.pallas_call(
        reflect_kernel,
        out_shape=(struct(rows, size), struct(cols, size)),
        in_specs=[SCALARS, WHOLE, WHOLE, WHOLE, pl.BlockSpec(memory_space=pl.ANY)],
        compiler_params=ROOM,
        cost_estimate=cost(4 * rows * size * size, 8 * rows * size),
    )(place, panel_rows, chunks, packed, coupling)
    coupling = exchange(coupling)
    rest = flip(part)
    extent = ratio * size * max(1, column_blocks // CLOSING)
    banded = pl.pallas_call(
        close_kernel,
        grid=(rows // extent,),
        out_shape=struct(rows, column_blocks, size),
        in_specs=[
            SCALARS,
            pl.BlockSpec((extent, cols), lambda i: (i, 0)),
            entire(at_cols),
            entire(reflect_cols),
            entire(part),
            entire(rest),
            entire(coupling),
            pl.BlockSpec((extent, size), lambda i: (i, 0)),
            pl.BlockSpec((size, size), lambda i: (4, 0)),
            pl.BlockSpec((size, size), lambda i: (5, 0)),
        ],
        out_specs=pl.BlockSpec((extent, column_blocks, size), lambda i: (i, 0, 0)),
        scratch_shapes=[
            pltpu.VMEM((cols, 2 * size), jnp.bfloat16),
            pltpu.VMEM((cols, 2 * size), jnp.bfloat16),
        ],
        compiler_params=MORE,
        cost_estimate=cost(4 * rows * cols * size, 8 * rows * cols),
    )(place, local_part, at_cols, reflect_cols, part, rest, coupling, reflect_rows, packed, packed)
    return (
        banded.reshape(matrix.shape),
        reflect_rows.reshape(local_blocks, 1, size, size),
    )


def solution(mesh):
    in_specs = (P(None, "row", None, None, "col", None),)
    out_specs = (P(None, "row", None, None, "col", None), P(None, "row", None, None))
    return jax.shard_map(
        on_device, mesh=mesh, in_specs=in_specs, out_specs=out_specs, check_vma=False
    )
```

```python
import functools
import jax
import jax.numpy as jnp
from jax import lax
from jax.experimental import pallas as pl
from jax.experimental.pallas import tpu as pltpu
from jax.sharding import Mesh, PartitionSpec as P

CLOSING = 2
COL = ("pair", "core")


def product(first, second, first_dim=1, second_dim=0):
    return lax.dot_general(
        first,
        second,
        (((first_dim,), (second_dim,)), ((), ())),
        precision=lax.Precision.HIGHEST,
        preferred_element_type=jnp.float32,
    )


def halves(array):
    high = array.astype(jnp.bfloat16)
    return high, (array - high.astype(jnp.float32)).astype(jnp.bfloat16)


def passes(first, second, first_dim=1, second_dim=0):
    dims = (((first_dim,), (second_dim,)), ((), ()))

    def one(a, b):
        return lax.dot_general(a, b, dims, preferred_element_type=jnp.float32)

    return one(first[0], second[0]) + (one(first[0], second[1]) + one(first[1], second[0]))


def factor_kernel(base_ref, out_ref):
    size = base_ref.shape[1]
    lane = lax.broadcasted_iota(jnp.int32, (1, size), 1)
    lane2 = lax.broadcasted_iota(jnp.int32, (1, 2 * size), 1)
    place = lax.broadcasted_iota(jnp.int32, (size, 1), 0)
    eye = (lane == place).astype(jnp.float32)
    g = jnp.concatenate([base_ref[:size], eye], axis=1)
    w = base_ref[size:]
    e = eye
    m = eye
    band = jnp.zeros((size, size), jnp.float32)
    turned = jnp.zeros((size, size), jnp.float32)
    for i in range(size):
        below = place > i
        here = place == i
        pivot = g[i : i + 1, i : i + 1]
        root = lax.rsqrt(pivot)
        root = root * (1.5 - 0.5 * pivot * root * root)
        row = jnp.where(lane2 >= i, g[i : i + 1, :] * root, 0.0)
        g = g - jnp.where(below, g[:, i : i + 1] * root, 0.0) * row
        r_row = row[:, :size]
        w_pivot = w[i : i + 1, i : i + 1]
        sign = jnp.where(w_pivot >= 0.0, -1.0, 1.0)
        inverse = 1.0 / (w_pivot - sign * (pivot * root))
        s_row = sign * r_row
        t_row = jnp.where(lane >= i, w[i : i + 1, :], 0.0) - s_row
        l = jnp.where(below, w[:, i : i + 1] * inverse, 0.0)
        w = w - jnp.where(here, s_row, l * t_row)
        w = jnp.where((lane == i) & below, l, w)
        e = e - l * e[i : i + 1, :]
        band = jnp.where(here, s_row, band)
        turned = jnp.where(here, sign * row[:, size:], turned)
        m_column = m[:, i : i + 1] * inverse
        m = jnp.where(lane == i, m_column, m - m_column * t_row)
    upper = jnp.where(lane >= place, w, 0.0)
    triangle = -product(upper, product(e, turned), 1, 1)
    out_ref[:size] = product(m, triangle)
    out_ref[size : 2 * size] = -product(product(band, m), triangle)
    out_ref[2 * size : 3 * size] = m
    out_ref[3 * size : 4 * size] = jnp.where(place > lane, w, 0.0) + eye
    out_ref[4 * size : 5 * size] = triangle
    out_ref[5 * size :] = band


def open_kernel(place, own_ref, other_ref, out_ref):
    size = own_ref.shape[1]
    count, extent, _ = out_ref.shape
    thin = size // count
    mine = extent - 2 * thin
    core = place[1]
    panel = jnp.where(core == 0, own_ref[...], other_ref[...])
    second = jnp.where((place[0] == 1) & (core == 0), panel[:size], 0.0)
    index = lax.broadcasted_iota(jnp.int32, panel.shape, 0)
    panel = jnp.where((index < size) & (place[0] == 0) & (core == 0), 0.0, panel)
    out_ref[:, :mine, :] = panel.reshape(count, mine, size)
    out_ref[:, mine : mine + thin, :] = product(panel, panel, 0, 0).reshape(count, thin, size)
    out_ref[:, mine + thin :, :] = second.reshape(count, thin, size)


def strip_kernel(place, matrix_ref, table_ref, out_ref):
    size = matrix_ref.shape[2]
    blocks = matrix_ref.shape[1]
    count, mine, _ = out_ref.shape
    each = size // mine
    for b in range(blocks):
        table_ref[:, b * size : (b + 1) * size] = matrix_ref[:, b, :]

    @pl.when(pl.program_id(0) == 0)
    def _():
        for b in range(blocks):
            turned = matrix_ref[:size, b, :].T
            if b == 0:
                turned = jnp.where(place[1] == 0, 0.0, turned)
            out_ref[b * each : (b + 1) * each] = turned.reshape(each, mine, size)


def image_kernel(
    place, own_ref, other_ref, matrix_ref, chunk_ref, out_ref, panel_ref, base_ref
):
    size = own_ref.shape[2]
    count, extent, _ = out_ref.shape
    mine = extent // 2
    each = size // mine
    own = own_ref[:, :mine, :].reshape(-1, size)
    other = other_ref[:, :mine, :].reshape(-1, size)
    even = place[1] % 2 == 0
    panel = jnp.concatenate([jnp.where(even, own, other), jnp.where(even, other, own)], axis=0)
    panel_ref[...] = panel
    both = own_ref[:, mine:, :] + other_ref[:, mine:, :]
    thin = both.shape[1] // 2
    base_ref[:size] = both[:, :thin].reshape(size, size)
    base_ref[size:] = both[:, thin:].reshape(size, size)
    high, low = halves(panel.T)
    matrix_high, matrix_low = halves(matrix_ref[...])
    image = jnp.dot(
        jnp.concatenate([high, low], axis=0), matrix_high, preferred_element_type=jnp.float32
    )
    image = image[:size] + (
        image[size:] + jnp.dot(high, matrix_low, preferred_element_type=jnp.float32)
    )
    for b in range(matrix_ref.shape[1] // size):
        turned = image[:, b * size : (b + 1) * size].T
        out_ref[b * each : (b + 1) * each, :mine, :] = turned.reshape(each, mine, size)
    out_ref[:, mine:, :] = jnp.broadcast_to(chunk_ref[...][None], (count, mine, size))


def middle_kernel(place, found_ref, panel_ref, second_ref, factors_ref, out_ref, scaled_ref):
    size = factors_ref.shape[1]
    count, extent, _ = found_ref.shape
    mine = extent // 2
    wide = size // count
    image = found_ref[0, :mine, :]
    for p in range(1, count):
        image = image + found_ref[p, :mine, :]
    block = (place[0] * mine) // size * place[3] + place[1]
    both = jnp.concatenate([image, second_ref[...]], axis=1)
    scaled = product(both, factors_ref[: 2 * size])
    scaled = jnp.where(block == 0, 0.0, scaled)
    reflect = product(panel_ref[...], factors_ref[2 * size : 3 * size])
    offset = pl.multiple_of(3 * size + (place[0] * mine) % size, mine)
    reflect = jnp.where(block == 1, factors_ref[pl.ds(offset, mine), :], reflect)
    reflect = jnp.where(block == 0, 0.0, reflect)
    coupling = product(reflect, scaled, 0, 0)
    scaled_ref[...] = scaled
    out_ref[:, :mine, :] = jnp.broadcast_to(scaled[None], (count, mine, size))
    out_ref[:, mine:, :] = coupling.reshape(count, wide, size)


def gather_kernel(found_ref, scaled_ref, out_ref):
    mine = scaled_ref.shape[0]
    count = out_ref.shape[0]
    out_ref[:, :mine, :] = jnp.broadcast_to(scaled_ref[...][None], (count,) + scaled_ref.shape)
    pieces = found_ref[:, mine:, :].sum(axis=0)
    out_ref[:, mine:, :] = jnp.broadcast_to(pieces[None], (count,) + pieces.shape)


def coupling_kernel(part_ref, out_ref, scaled_ref):
    mine = scaled_ref.shape[1]
    scaled_ref[...] = part_ref[:, :mine, :]
    pieces = part_ref[:, mine:, :].sum(axis=0)
    out_ref[...] = jnp.broadcast_to(pieces[None], out_ref.shape)


def reflect_kernel(
    place,
    panel_ref,
    chunks_ref,
    factors_ref,
    ready_ref,
    rows_ref,
    cols_ref,
    high_ref,
    low_ref,
):
    del ready_ref
    size = factors_ref.shape[1]
    mine = chunks_ref.shape[1] // 2
    inverse = factors_ref[2 * size : 3 * size]
    unit_lower = factors_ref[3 * size : 4 * size]
    rows_ref[...] = product(panel_ref[...], inverse)
    cols_ref[...] = product(chunks_ref[:, mine:, :].reshape(-1, size), inverse)

    @pl.when(place[0] == 1)
    def _():
        rows_ref[:size] = unit_lower

    @pl.when(place[1] == 1)
    def _():
        cols_ref[:size] = unit_lower

    triangle = halves(factors_ref[4 * size : 5 * size])
    high, low = halves(passes(halves(cols_ref[...]), triangle, 1, 1))
    high_ref[...] = high
    low_ref[...] = low


def close_kernel(
    place,
    matrix_ref,
    cols_ref,
    reflect_cols_ref,
    own_ref,
    other_ref,
    coupling_ref,
    reflect_ref,
    turned_high_ref,
    turned_low_ref,
    band_ref,
    out_ref,
    high,
    low,
):
    step = pl.program_id(0)
    size = band_ref.shape[1]
    mine = own_ref.shape[1]
    blocks = out_ref.shape[1]
    extent = out_ref.shape[0]
    parts = size // mine
    pairs, count = own_ref.shape[0], cols_ref.shape[0]
    ratio = 2 * pairs // count

    @pl.when(step == 0)
    def _():
        cores = coupling_ref[...].reshape(-1, 2, coupling_ref.shape[1], size)
        coupling = halves((cores[:, 0] + cores[:, 1]).reshape(size, size))
        scaled_cols = cols_ref[:, :mine, :].reshape(-1, size)
        update = scaled_cols - passes((turned_high_ref[...], turned_low_ref[...]), coupling)
        right = halves(jnp.concatenate([update, reflect_cols_ref[...]], axis=1))
        high[...] = right[0]
        low[...] = right[1]

    scaled = []
    for k in range(extent // mine):
        block, part = divmod(k, parts)
        source = (step * (extent // size // ratio) + block // ratio) * parts + part
        col = block % ratio * count + lax.rem(source + count // 2, count)
        here = lax.rem(col, 2) == lax.rem(place[1], 2)
        at = lax.div(col, 2)
        scaled.append(jnp.where(here, own_ref[at], other_ref[at]))
    left = jnp.concatenate([reflect_ref[...], jnp.concatenate(scaled, axis=0)], axis=1)
    value = matrix_ref[...] - passes(halves(left), (high[...], low[...]), 1, 1)
    band = band_ref[...]
    for h in range(extent // size):
        row_block = (step * (extent // size) + h) * place[2] + place[0]
        for b in range(blocks):
            column_block = b * place[3] + place[1]
            tile = value[h * size : (h + 1) * size, b * size : (b + 1) * size]
            if b == 0:
                rim = jnp.where(row_block == 1, band, 0.0)
                tile = jnp.where((column_block == 0) & (row_block >= 1), rim, tile)
            if h == 0:
                rim = jnp.where(column_block == 1, band.T, 0.0) if b == 0 else jnp.zeros_like(band)
                tile = jnp.where((row_block == 0) & (column_block >= 1), rim, tile)
            out_ref[h * size : (h + 1) * size, b, :] = tile


def cost(flops, moved):
    return pl.CostEstimate(flops=flops, bytes_accessed=moved, transcendentals=0)


def struct(*shape):
    return jax.ShapeDtypeStruct(shape, jnp.float32)


SCALARS = pl.BlockSpec(memory_space=pltpu.SMEM)
WHOLE = pl.BlockSpec(memory_space=pltpu.VMEM)


def entire(array):
    return pl.BlockSpec(array.shape, lambda i: (0,) * array.ndim)


ROOM = pltpu.CompilerParams(vmem_limit_bytes=24 << 20)
MORE = pltpu.CompilerParams(vmem_limit_bytes=56 << 20)


def factors(base):
    size = base.shape[1]
    return pl.pallas_call(
        factor_kernel,
        out_shape=struct(6 * size, size),
        compiler_params=ROOM,
        cost_estimate=cost(1 << 28, 1 << 25),
    )(base)


def exchange(array, axis):
    return lax.all_to_all(array, axis, 0, 0)


def flip(array):
    return lax.ppermute(array, "core", [(0, 1), (1, 0)])


def to_all(array, count):
    return jnp.broadcast_to(array[None], (count,) + array.shape)


def to_rows(chunk):
    rows_count = lax.axis_size("row")
    cols_count = lax.axis_size(COL)
    pairs = []
    for row in range(rows_count):
        for col in range(cols_count):
            half, k = divmod(col, rows_count)
            source = (k + rows_count // 2) % rows_count * cols_count + half * rows_count + row
            pairs.append((source, row * cols_count + col))
    return lax.ppermute(chunk, ("row",) + COL, pairs)


def on_device(matrix):
    rows_count = lax.axis_size("row")
    cols_count = lax.axis_size(COL)
    row_place = lax.axis_index("row")
    col_place = lax.axis_index(COL)
    local_blocks = matrix.shape[0]
    size = matrix.shape[2]
    column_blocks = matrix.shape[3]
    rows = local_blocks * size
    cols = column_blocks * size
    ratio = cols_count // rows_count
    pairs = cols_count // 2
    mine = rows // cols_count
    thin = size // pairs
    wide = size // rows_count
    table = matrix.reshape(rows, column_blocks, size)
    place = jnp.stack(
        [row_place, col_place, jnp.int32(rows_count), jnp.int32(cols_count)]
    ).astype(jnp.int32)

    panel = table[:, 0, :]
    opening = pl.pallas_call(
        open_kernel,
        out_shape=struct(pairs, mine + 2 * thin, size),
        in_specs=[SCALARS, WHOLE, WHOLE],
        compiler_params=ROOM,
        cost_estimate=cost(rows * size * size, 8 * rows * size),
    )(place, panel[: rows // 2], lax.ppermute(panel[rows // 2 :], COL, [(0, 1)]))
    found = exchange(opening, "pair")[0]
    local_part, strip = pl.pallas_call(
        strip_kernel,
        grid=(column_blocks,),
        out_shape=(struct(rows, cols), struct(rows_count, mine, size)),
        in_specs=[
            SCALARS,
            pl.BlockSpec((rows // column_blocks, column_blocks, size), lambda i: (i, 0, 0)),
        ],
        out_specs=(
            pl.BlockSpec((rows // column_blocks, cols), lambda i: (i, 0)),
            pl.BlockSpec((rows_count, mine, size), lambda i: (0, 0, 0)),
        ),
        compiler_params=ROOM,
        cost_estimate=cost(0, 8 * rows * cols),
    )(place, table)
    summed = exchange(
        jnp.concatenate([strip, to_all(found[mine:], rows_count)], axis=1), "row"
    )
    panel_chunk = summed[0, :mine]
    second_chunk = summed[1, :mine]
    square = summed[:, mine:].sum(axis=0)
    own = exchange(to_all(jnp.concatenate([found[:mine], square], axis=0), pairs), "pair")
    other = flip(own)

    images, panel_rows, base = pl.pallas_call(
        image_kernel,
        out_shape=(struct(rows_count, 2 * mine, size), struct(rows, size), struct(2 * size, size)),
        in_specs=[SCALARS, WHOLE, WHOLE, WHOLE, WHOLE],
        compiler_params=ROOM,
        cost_estimate=cost(2 * rows * cols * size, 4 * rows * (cols + 3 * size)),
    )(place, own, other, local_part, panel_chunk)
    chunks = exchange(images, "row")
    packed = factors(base)

    middle, scaled = pl.pallas_call(
        middle_kernel,
        out_shape=(struct(rows_count, mine + wide, size), struct(mine, size)),
        in_specs=[SCALARS, WHOLE, WHOLE, WHOLE, WHOLE],
        compiler_params=ROOM,
        cost_estimate=cost(2 * mine * size * size * 5, 8 * rows * size),
    )(place, chunks, panel_chunk, second_chunk, packed)
    scaled = to_rows(scaled)
    at_cols = exchange(middle, "row")

    gathering = pl.pallas_call(
        gather_kernel,
        out_shape=struct(pairs, mine + wide, size),
        compiler_params=ROOM,
        cost_estimate=cost(0, 4 * rows * size),
    )(at_cols, scaled)
    part = exchange(gathering, "pair")
    sums, part = pl.pallas_call(
        coupling_kernel,
        out_shape=(struct(2 * rows_count, wide, size), struct(pairs, mine, size)),
        compiler_params=ROOM,
        cost_estimate=cost(0, 4 * rows * size),
    )(part)
    coupling = exchange(sums, ("row", "core"))
    halved = jax.ShapeDtypeStruct((cols, size), jnp.bfloat16)
    reflect_rows, reflect_cols, high, low = pl.pallas_call(
        reflect_kernel,
        out_shape=(struct(rows, size), struct(cols, size), halved, halved),
        in_specs=[SCALARS, WHOLE, WHOLE, WHOLE, pl.BlockSpec(memory_space=pl.ANY)],
        compiler_params=ROOM,
        cost_estimate=cost(4 * rows * size * size, 8 * rows * size),
    )(place, panel_rows, chunks, packed, sums)
    rest = flip(part)
    extent = ratio * size * max(1, column_blocks // CLOSING)
    banded = pl.pallas_call(
        close_kernel,
        grid=(rows // extent,),
        out_shape=struct(rows, column_blocks, size),
        in_specs=[
            SCALARS,
            pl.BlockSpec((extent, cols), lambda i: (i, 0)),
            entire(at_cols),
            entire(reflect_cols),
            entire(part),
            entire(rest),
            WHOLE,
            pl.BlockSpec((extent, size), lambda i: (i, 0)),
            entire(high),
            entire(low),
            pl.BlockSpec((size, size), lambda i: (5, 0)),
        ],
        out_specs=pl.BlockSpec((extent, column_blocks, size), lambda i: (i, 0, 0)),
        scratch_shapes=[
            pltpu.VMEM((cols, 2 * size), jnp.bfloat16),
            pltpu.VMEM((cols, 2 * size), jnp.bfloat16),
        ],
        compiler_params=MORE,
        cost_estimate=cost(4 * rows * cols * size, 8 * rows * cols),
    )(
        place,
        local_part,
        at_cols,
        reflect_cols,
        part,
        rest,
        coupling,
        reflect_rows,
        high,
        low,
        packed,
    )
    return (
        banded.reshape(matrix.shape),
        reflect_rows.reshape(local_blocks, 1, size, size),
    )


def solution(mesh):
    rows_count, cols_count = mesh.devices.shape
    devices = mesh.devices.reshape(rows_count, cols_count // 2, 2)
    in_specs = (P(None, "row", None, None, COL, None),)
    out_specs = (P(None, "row", None, None, COL, None), P(None, "row", None, None))
    return jax.shard_map(
        on_device,
        mesh=Mesh(devices, ("row",) + COL),
        in_specs=in_specs,
        out_specs=out_specs,
        check_vma=False,
    )
```

```python
import functools
import jax
import jax.numpy as jnp
from jax import lax
from jax.experimental import pallas as pl
from jax.experimental.pallas import tpu as pltpu
from jax.sharding import Mesh, PartitionSpec as P

CLOSING = 2
COL = ("pair", "core")


def product(first, second, first_dim=1, second_dim=0):
    return lax.dot_general(
        first,
        second,
        (((first_dim,), (second_dim,)), ((), ())),
        precision=lax.Precision.HIGHEST,
        preferred_element_type=jnp.float32,
    )


def halves(array):
    high = array.astype(jnp.bfloat16)
    return high, (array - high.astype(jnp.float32)).astype(jnp.bfloat16)


def passes(first, second, first_dim=1, second_dim=0):
    dims = (((first_dim,), (second_dim,)), ((), ()))

    def one(a, b):
        return lax.dot_general(a, b, dims, preferred_element_type=jnp.float32)

    return one(first[0], second[0]) + (one(first[0], second[1]) + one(first[1], second[0]))


def factor_kernel(base_ref, out_ref):
    size = base_ref.shape[1]
    lane = lax.broadcasted_iota(jnp.int32, (1, size), 1)
    lane2 = lax.broadcasted_iota(jnp.int32, (1, 2 * size), 1)
    place = lax.broadcasted_iota(jnp.int32, (size, 1), 0)
    eye = (lane == place).astype(jnp.float32)
    g = jnp.concatenate([base_ref[:size], eye], axis=1)
    w = base_ref[size:]
    e = eye
    m = eye
    band = jnp.zeros((size, size), jnp.float32)
    turned = jnp.zeros((size, size), jnp.float32)
    for i in range(size):
        below = place > i
        here = place == i
        pivot = g[i : i + 1, i : i + 1]
        root = lax.rsqrt(pivot)
        root = root * (1.5 - 0.5 * pivot * root * root)
        row = jnp.where(lane2 >= i, g[i : i + 1, :] * root, 0.0)
        g = g - jnp.where(below, g[:, i : i + 1] * root, 0.0) * row
        r_row = row[:, :size]
        w_pivot = w[i : i + 1, i : i + 1]
        sign = jnp.where(w_pivot >= 0.0, -1.0, 1.0)
        inverse = 1.0 / (w_pivot - sign * (pivot * root))
        s_row = sign * r_row
        t_row = jnp.where(lane >= i, w[i : i + 1, :], 0.0) - s_row
        l = jnp.where(below, w[:, i : i + 1] * inverse, 0.0)
        w = w - jnp.where(here, s_row, l * t_row)
        w = jnp.where((lane == i) & below, l, w)
        e = e - l * e[i : i + 1, :]
        band = jnp.where(here, s_row, band)
        turned = jnp.where(here, sign * row[:, size:], turned)
        m_column = m[:, i : i + 1] * inverse
        m = jnp.where(lane == i, m_column, m - m_column * t_row)
    upper = jnp.where(lane >= place, w, 0.0)
    triangle = -product(upper, product(e, turned), 1, 1)
    out_ref[:size] = product(m, triangle)
    out_ref[size : 2 * size] = -product(product(band, m), triangle)
    out_ref[2 * size : 3 * size] = m
    out_ref[3 * size : 4 * size] = jnp.where(place > lane, w, 0.0) + eye
    out_ref[4 * size : 5 * size] = triangle
    out_ref[5 * size :] = band


def open_kernel(place, own_ref, other_ref, out_ref):
    size = own_ref.shape[1]
    count, extent, _ = out_ref.shape
    thin = size // count
    mine = extent - 2 * thin
    core = place[1]
    panel = jnp.where(core == 0, own_ref[...], other_ref[...])
    second = jnp.where((place[0] == 1) & (core == 0), panel[:size], 0.0)
    index = lax.broadcasted_iota(jnp.int32, panel.shape, 0)
    panel = jnp.where((index < size) & (place[0] == 0) & (core == 0), 0.0, panel)
    out_ref[:, :mine, :] = panel.reshape(count, mine, size)
    out_ref[:, mine : mine + thin, :] = product(panel, panel, 0, 0).reshape(count, thin, size)
    out_ref[:, mine + thin :, :] = second.reshape(count, thin, size)


def strip_kernel(place, matrix_ref, table_ref, out_ref):
    size = matrix_ref.shape[2]
    blocks = matrix_ref.shape[1]
    count, mine, _ = out_ref.shape
    each = size // mine
    for b in range(blocks):
        table_ref[:, b * size : (b + 1) * size] = matrix_ref[:, b, :]

    @pl.when(pl.program_id(0) == 0)
    def _():
        for b in range(blocks):
            turned = matrix_ref[:size, b, :].T
            if b == 0:
                turned = jnp.where(place[1] == 0, 0.0, turned)
            out_ref[b * each : (b + 1) * each] = turned.reshape(each, mine, size)


def image_kernel(
    place, own_ref, other_ref, matrix_ref, chunk_ref, out_ref, panel_ref, base_ref
):
    size = own_ref.shape[2]
    count, extent, _ = out_ref.shape
    mine = extent // 2
    each = size // mine
    own = own_ref[:, :mine, :].reshape(-1, size)
    other = other_ref[:, :mine, :].reshape(-1, size)
    even = place[1] % 2 == 0
    panel = jnp.concatenate([jnp.where(even, own, other), jnp.where(even, other, own)], axis=0)
    panel_ref[...] = panel
    both = own_ref[:, mine:, :] + other_ref[:, mine:, :]
    thin = both.shape[1] // 2
    base_ref[:size] = both[:, :thin].reshape(size, size)
    base_ref[size:] = both[:, thin:].reshape(size, size)
    high, low = halves(panel.T)
    matrix_high, matrix_low = halves(matrix_ref[...])
    image = jnp.dot(
        jnp.concatenate([high, low], axis=0), matrix_high, preferred_element_type=jnp.float32
    )
    image = image[:size] + (
        image[size:] + jnp.dot(high, matrix_low, preferred_element_type=jnp.float32)
    )
    for b in range(matrix_ref.shape[1] // size):
        turned = image[:, b * size : (b + 1) * size].T
        out_ref[b * each : (b + 1) * each, :mine, :] = turned.reshape(each, mine, size)
    out_ref[:, mine:, :] = jnp.broadcast_to(chunk_ref[...][None], (count, mine, size))


def middle_kernel(place, found_ref, panel_ref, second_ref, factors_ref, out_ref, scaled_ref):
    size = factors_ref.shape[1]
    count, extent, _ = found_ref.shape
    mine = extent // 2
    wide = size // count
    image = found_ref[0, :mine, :]
    for p in range(1, count):
        image = image + found_ref[p, :mine, :]
    block = (place[0] * mine) // size * place[3] + place[1]
    both = jnp.concatenate([image, second_ref[...]], axis=1)
    scaled = product(both, factors_ref[: 2 * size])
    scaled = jnp.where(block == 0, 0.0, scaled)
    reflect = product(panel_ref[...], factors_ref[2 * size : 3 * size])
    offset = pl.multiple_of(3 * size + (place[0] * mine) % size, mine)
    reflect = jnp.where(block == 1, factors_ref[pl.ds(offset, mine), :], reflect)
    reflect = jnp.where(block == 0, 0.0, reflect)
    coupling = product(reflect, scaled, 0, 0)
    scaled_ref[...] = scaled
    out_ref[:, :mine, :] = jnp.broadcast_to(scaled[None], (count, mine, size))
    out_ref[:, mine:, :] = coupling.reshape(count, wide, size)


def gather_kernel(found_ref, scaled_ref, out_ref):
    mine = scaled_ref.shape[0]
    count = out_ref.shape[0]
    out_ref[:, :mine, :] = jnp.broadcast_to(scaled_ref[...][None], (count,) + scaled_ref.shape)
    pieces = found_ref[:, mine:, :].sum(axis=0)
    out_ref[:, mine:, :] = jnp.broadcast_to(pieces[None], (count,) + pieces.shape)


def coupling_kernel(part_ref, out_ref, scaled_ref):
    mine = scaled_ref.shape[1]
    scaled_ref[...] = part_ref[:, :mine, :]
    pieces = part_ref[:, mine:, :].sum(axis=0)
    out_ref[...] = jnp.broadcast_to(pieces[None], out_ref.shape)


def reflect_kernel(
    place,
    panel_ref,
    chunks_ref,
    factors_ref,
    ready_ref,
    rows_ref,
    cols_ref,
    high_ref,
    low_ref,
):
    del ready_ref
    size = factors_ref.shape[1]
    mine = chunks_ref.shape[1] // 2
    inverse = factors_ref[2 * size : 3 * size]
    unit_lower = factors_ref[3 * size : 4 * size]
    rows_ref[...] = product(panel_ref[...], inverse)
    cols_ref[...] = product(chunks_ref[:, mine:, :].reshape(-1, size), inverse)

    @pl.when(place[0] == 1)
    def _():
        rows_ref[:size] = unit_lower

    @pl.when(place[1] == 1)
    def _():
        cols_ref[:size] = unit_lower

    triangle = halves(factors_ref[4 * size : 5 * size])
    high, low = halves(passes(halves(cols_ref[...]), triangle, 1, 1))
    high_ref[...] = high
    low_ref[...] = low


def close_kernel(
    place,
    matrix_ref,
    cols_ref,
    reflect_cols_ref,
    own_ref,
    other_ref,
    coupling_ref,
    reflect_ref,
    turned_high_ref,
    turned_low_ref,
    band_ref,
    out_ref,
    high,
    low,
):
    step = pl.program_id(0)
    size = band_ref.shape[1]
    mine = own_ref.shape[1]
    blocks = out_ref.shape[1]
    extent = out_ref.shape[0]
    parts = size // mine
    pairs, count = own_ref.shape[0], cols_ref.shape[0]
    ratio = 2 * pairs // count

    @pl.when(step == 0)
    def _():
        cores = coupling_ref[...].reshape(-1, 2, coupling_ref.shape[1], size)
        coupling = halves((cores[:, 0] + cores[:, 1]).reshape(size, size))
        scaled_cols = cols_ref[:, :mine, :].reshape(-1, size)
        update = scaled_cols - passes((turned_high_ref[...], turned_low_ref[...]), coupling)
        right = halves(jnp.concatenate([update, reflect_cols_ref[...]], axis=1))
        high[...] = right[0]
        low[...] = right[1]

    scaled = []
    for k in range(extent // mine):
        block, part = divmod(k, parts)
        source = (step * (extent // size // ratio) + block // ratio) * parts + part
        col = block % ratio * count + lax.rem(source + count // 2, count)
        here = lax.rem(col, 2) == lax.rem(place[1], 2)
        at = lax.div(col, 2)
        scaled.append(jnp.where(here, own_ref[at], other_ref[at]))
    left = jnp.concatenate([reflect_ref[...], jnp.concatenate(scaled, axis=0)], axis=1)
    value = matrix_ref[...] - passes(halves(left), (high[...], low[...]), 1, 1)
    band = band_ref[...]
    for h in range(extent // size):
        row_block = (step * (extent // size) + h) * place[2] + place[0]
        for b in range(blocks):
            column_block = b * place[3] + place[1]
            tile = value[h * size : (h + 1) * size, b * size : (b + 1) * size]
            if b == 0:
                rim = jnp.where(row_block == 1, band, 0.0)
                tile = jnp.where((column_block == 0) & (row_block >= 1), rim, tile)
            if h == 0:
                rim = jnp.where(column_block == 1, band.T, 0.0) if b == 0 else jnp.zeros_like(band)
                tile = jnp.where((row_block == 0) & (column_block >= 1), rim, tile)
            out_ref[h * size : (h + 1) * size, b, :] = tile


def cost(flops, moved):
    return pl.CostEstimate(flops=flops, bytes_accessed=moved, transcendentals=0)


def struct(*shape):
    return jax.ShapeDtypeStruct(shape, jnp.float32)


SCALARS = pl.BlockSpec(memory_space=pltpu.SMEM)
WHOLE = pl.BlockSpec(memory_space=pltpu.VMEM)


def entire(array):
    return pl.BlockSpec(array.shape, lambda i: (0,) * array.ndim)


ROOM = pltpu.CompilerParams(vmem_limit_bytes=24 << 20)
MORE = pltpu.CompilerParams(vmem_limit_bytes=50 << 20)


def factors(base):
    size = base.shape[1]
    return pl.pallas_call(
        factor_kernel,
        out_shape=struct(6 * size, size),
        compiler_params=ROOM,
        cost_estimate=cost(1 << 28, 1 << 25),
    )(base)


def exchange(array, axis):
    return lax.all_to_all(array, axis, 0, 0)


def flip(array):
    return lax.ppermute(array, "core", [(0, 1), (1, 0)])


def to_all(array, count):
    return jnp.broadcast_to(array[None], (count,) + array.shape)


def to_rows(chunk):
    rows_count = lax.axis_size("row")
    cols_count = lax.axis_size(COL)
    pairs = []
    for row in range(rows_count):
        for col in range(cols_count):
            half, k = divmod(col, rows_count)
            source = (k + rows_count // 2) % rows_count * cols_count + half * rows_count + row
            pairs.append((source, row * cols_count + col))
    return lax.ppermute(chunk, ("row",) + COL, pairs)


def on_device(matrix):
    rows_count = lax.axis_size("row")
    cols_count = lax.axis_size(COL)
    row_place = lax.axis_index("row")
    col_place = lax.axis_index(COL)
    local_blocks = matrix.shape[0]
    size = matrix.shape[2]
    column_blocks = matrix.shape[3]
    rows = local_blocks * size
    cols = column_blocks * size
    ratio = cols_count // rows_count
    pairs = cols_count // 2
    mine = rows // cols_count
    thin = size // pairs
    wide = size // rows_count
    table = matrix.reshape(rows, column_blocks, size)
    place = jnp.stack(
        [row_place, col_place, jnp.int32(rows_count), jnp.int32(cols_count)]
    ).astype(jnp.int32)

    panel = table[:, 0, :]
    opening = pl.pallas_call(
        open_kernel,
        out_shape=struct(pairs, mine + 2 * thin, size),
        in_specs=[SCALARS, WHOLE, WHOLE],
        compiler_params=ROOM,
        cost_estimate=cost(rows * size * size, 8 * rows * size),
    )(place, panel[: rows // 2], lax.ppermute(panel[rows // 2 :], COL, [(0, 1)]))
    found = exchange(opening, "pair")[0]
    local_part, strip = pl.pallas_call(
        strip_kernel,
        grid=(column_blocks,),
        out_shape=(struct(rows, cols), struct(rows_count, mine, size)),
        in_specs=[
            SCALARS,
            pl.BlockSpec((rows // column_blocks, column_blocks, size), lambda i: (i, 0, 0)),
        ],
        out_specs=(
            pl.BlockSpec((rows // column_blocks, cols), lambda i: (i, 0)),
            pl.BlockSpec((rows_count, mine, size), lambda i: (0, 0, 0)),
        ),
        compiler_params=ROOM,
        cost_estimate=cost(0, 8 * rows * cols),
    )(place, table)
    summed = exchange(
        jnp.concatenate([strip, to_all(found[mine:], rows_count)], axis=1), "row"
    )
    panel_chunk = summed[0, :mine]
    second_chunk = summed[1, :mine]
    square = summed[:, mine:].sum(axis=0)
    own = exchange(to_all(jnp.concatenate([found[:mine], square], axis=0), pairs), "pair")
    other = flip(own)

    images, panel_rows, base = pl.pallas_call(
        image_kernel,
        out_shape=(struct(rows_count, 2 * mine, size), struct(rows, size), struct(2 * size, size)),
        in_specs=[SCALARS, WHOLE, WHOLE, WHOLE, WHOLE],
        compiler_params=ROOM,
        cost_estimate=cost(2 * rows * cols * size, 4 * rows * (cols + 3 * size)),
    )(place, own, other, local_part, panel_chunk)
    chunks = exchange(images, "row")
    packed = factors(base)

    middle, scaled = pl.pallas_call(
        middle_kernel,
        out_shape=(struct(rows_count, mine + wide, size), struct(mine, size)),
        in_specs=[SCALARS, WHOLE, WHOLE, WHOLE, WHOLE],
        compiler_params=ROOM,
        cost_estimate=cost(2 * mine * size * size * 5, 8 * rows * size),
    )(place, chunks, panel_chunk, second_chunk, packed)
    scaled = to_rows(scaled)
    at_cols = exchange(middle, "row")

    gathering = pl.pallas_call(
        gather_kernel,
        out_shape=struct(pairs, mine + wide, size),
        compiler_params=ROOM,
        cost_estimate=cost(0, 4 * rows * size),
    )(at_cols, scaled)
    part = exchange(gathering, "pair")
    sums, part = pl.pallas_call(
        coupling_kernel,
        out_shape=(struct(2 * rows_count, wide, size), struct(pairs, mine, size)),
        compiler_params=ROOM,
        cost_estimate=cost(0, 4 * rows * size),
    )(part)
    coupling = exchange(sums, ("row", "core"))
    halved = jax.ShapeDtypeStruct((cols, size), jnp.bfloat16)
    reflect_rows, reflect_cols, high, low = pl.pallas_call(
        reflect_kernel,
        out_shape=(struct(rows, size), struct(cols, size), halved, halved),
        in_specs=[SCALARS, WHOLE, WHOLE, WHOLE, pl.BlockSpec(memory_space=pl.ANY)],
        compiler_params=ROOM,
        cost_estimate=cost(4 * rows * size * size, 8 * rows * size),
    )(place, panel_rows, chunks, packed, sums)
    rest = flip(part)
    extent = ratio * size * max(1, column_blocks // CLOSING)
    banded = pl.pallas_call(
        close_kernel,
        grid=(rows // extent,),
        out_shape=struct(rows, column_blocks, size),
        in_specs=[
            SCALARS,
            pl.BlockSpec((extent, cols), lambda i: (i, 0)),
            entire(at_cols),
            entire(reflect_cols),
            entire(part),
            entire(rest),
            WHOLE,
            pl.BlockSpec((extent, size), lambda i: (i, 0)),
            entire(high),
            entire(low),
            pl.BlockSpec((size, size), lambda i: (5, 0)),
        ],
        out_specs=pl.BlockSpec((extent, column_blocks, size), lambda i: (i, 0, 0)),
        scratch_shapes=[
            pltpu.VMEM((cols, 2 * size), jnp.bfloat16),
            pltpu.VMEM((cols, 2 * size), jnp.bfloat16),
        ],
        compiler_params=MORE,
        cost_estimate=cost(4 * rows * cols * size, 8 * rows * cols),
    )(
        place,
        local_part,
        at_cols,
        reflect_cols,
        part,
        rest,
        coupling,
        reflect_rows,
        high,
        low,
        packed,
    )
    return (
        banded.reshape(matrix.shape),
        reflect_rows.reshape(local_blocks, 1, size, size),
    )


def solution(mesh):
    rows_count, cols_count = mesh.devices.shape
    devices = mesh.devices.reshape(rows_count, cols_count // 2, 2)
    in_specs = (P(None, "row", None, None, COL, None),)
    out_specs = (P(None, "row", None, None, COL, None), P(None, "row", None, None))
    return jax.shard_map(
        on_device,
        mesh=Mesh(devices, ("row",) + COL),
        in_specs=in_specs,
        out_specs=out_specs,
        check_vma=False,
    )
```
